512 devices in a mesh: dp: 128 (over z_hi, y, x), feat: 4 (over z_lo, core).
Axes of the slice: x: 4, y: 8, z: 8 (z_hi: 4, z_lo: 2; z = z_hi * 2 + z_lo), core: 2. Of those that a mesh axis runs over, the one named last changes fastest.
Arguments:
- train_grads: bfloat16 [131072, 4096], P('dp', 'feat')
- token_counts: int32 [131072], P('dp'), may hold values from 1 to 1024, as said below
- train_ids: int32 [131072], P('dp'), may hold values from 0 to 49151
- query_grads: bfloat16 [24576, 4096], P('dp', 'feat')
- query_ids: int32 [24576], P('dp'), may hold values from 0 to 49151
Outputs:
- influence: float32 [4, 192, 131072], P(None, 'feat', 'dp')
The draws below stay inside these ranges and needn't reach their ends.
Inputs may be any that keep to these rules, and one draw needn't show every extreme that they name: `token_counts`: some training example has exactly 1024 tokens and some exactly one.
All inputs are finite; a program needn't handle non-finite values.
Results may differ from the reference program's by a relative error of at most 0.00115.
The reference program's roundings to bfloat16 on the way (of `features` and `preconditioned`) count: a program that leaves them out, or rounds other values in their place, can miss the bound.
Values may be sent and summed in bfloat16 or wider, within the bound.
A program may use at most 64 MiB of HBM per device.

```python
import jax
import jax.numpy as jnp
from jax import lax

KOUT = 64
KIN = 64
EX_DEV = 1024
Q_DEV = 192
STEPS = 4
MAX_TOKENS = 1024
FEATS = 4096
TRAIN = 131072
QUERIES = 24576
ID_RANGE = 49152
N_DP = 128


def scale_tables(key):
    row_key, col_key = jax.random.split(jax.random.fold_in(key, 101))
    row_scales = 10.0 ** jax.random.uniform(row_key, (KOUT,), jnp.float32, 0.0, 1.0)
    col_scales = 10.0 ** jax.random.uniform(col_key, (KIN,), jnp.float32, 0.0, 1.0)
    return (row_scales, col_scales)


def count_table(key):
    counts = jax.random.randint(jax.random.fold_in(key, 202), (TRAIN,), 1, MAX_TOKENS + 1)
    counts = counts.at[0].set(MAX_TOKENS).at[1].set(1)
    return counts.astype(jnp.int32)


def draw_token_counts(key, part):
    return count_table(key)


def draw_train_grads(key, part):
    row_scales, col_scales = scale_tables(key)
    counts = count_table(key).astype(jnp.float32)
    key = jax.random.fold_in(key, 3)
    first_key, second_key = jax.random.split(key, 2)
    normal_part = jax.random.normal(first_key, (TRAIN, KOUT, KIN), jnp.float32)
    spread = 10.0 ** jax.random.uniform(second_key, (TRAIN,), jnp.float32, -0.3, 0.3)
    rising = 1.0 + 2.0 * jnp.arange(TRAIN, dtype=jnp.float32) / TRAIN
    example_scale = spread * rising * counts
    values = normal_part * row_scales[None, :, None] * col_scales[None, None, :] * example_scale[:, None, None]
    return values.reshape(TRAIN, KOUT * KIN).astype(jnp.bfloat16)


def draw_query_grads(key, part):
    row_scales, col_scales = scale_tables(key)
    key = jax.random.fold_in(key, 7)
    first_key = jax.random.fold_in(key, 0)
    normal_part = jax.random.normal(first_key, (QUERIES, KOUT, KIN), jnp.float32)
    values = normal_part * row_scales[None, :, None] * col_scales[None, None, :] / 16.0
    return values.reshape(QUERIES, KOUT * KIN).astype(jnp.bfloat16)


def touch_ends(entries, own_key, smallest, high):
    longest = entries.shape.index(max(entries.shape))
    spots = []
    for shift in (0, 1):
        where = [jax.random.randint(jax.random.fold_in(own_key, axis), (), 0, length) for axis, length in enumerate(entries.shape)]
        where[longest] = (where[longest] + shift) % entries.shape[longest]
        spots.append(tuple(where))
    return entries.at[spots[0]].set(smallest).at[spots[1]].set(high)


def setup_inputs(seed: int = 0) -> dict:
    streams_of = jax.random.split(jax.random.key(seed), 6)
    train_grads = draw_train_grads(jax.random.fold_in(streams_of[5], 71), 0)
    token_counts = draw_token_counts(jax.random.fold_in(streams_of[5], 71), 0)
    train_ids = touch_ends(jax.random.randint(streams_of[2], (TRAIN,), 0, ID_RANGE), jax.random.fold_in(streams_of[2], 1), 0, ID_RANGE - 1).astype(jnp.int32)
    query_grads = draw_query_grads(jax.random.fold_in(streams_of[5], 71), 0)
    query_ids = touch_ends(jax.random.randint(streams_of[4], (QUERIES,), 0, ID_RANGE), jax.random.fold_in(streams_of[4], 1), 0, ID_RANGE - 1).astype(jnp.int32)
    return dict(train_grads=train_grads, token_counts=token_counts, train_ids=train_ids, query_grads=query_grads, query_ids=query_ids)


damping = 0.1

def reference(train_grads, token_counts, train_ids, query_grads, query_ids):
    features = (train_grads.astype(jnp.float32) / token_counts[:, None].astype(jnp.float32)).astype(jnp.bfloat16)
    blocks = features.reshape(N_DP, EX_DEV, KOUT, KIN)

    def add_block(totals, one_block):
        matrices = one_block.astype(jnp.float32)
        right_part = totals[0] + jnp.einsum('eab,eac->bc', matrices, matrices, precision=lax.Precision.HIGHEST)
        left_part = totals[1] + jnp.einsum('eab,ecb->ac', matrices, matrices, precision=lax.Precision.HIGHEST)
        return ((right_part, left_part), None)
    start_totals = (jnp.zeros((KIN, KIN), jnp.float32), jnp.zeros((KOUT, KOUT), jnp.float32))
    (right_factor, left_factor), _ = lax.scan(add_block, start_totals, blocks)
    mean_total = jnp.trace(right_factor) / TRAIN
    right_damped = right_factor / TRAIN + damping * mean_total / KIN * jnp.eye(KIN, dtype=jnp.float32)
    left_damped = left_factor / TRAIN + damping * mean_total / KOUT * jnp.eye(KOUT, dtype=jnp.float32)
    left_inv = jnp.linalg.solve(left_damped, jnp.eye(KOUT, dtype=jnp.float32))
    right_inv = jnp.linalg.solve(right_damped, jnp.eye(KIN, dtype=jnp.float32))
    queries = query_grads.astype(jnp.float32).reshape(QUERIES, KOUT, KIN)
    mixed_rows = jnp.einsum('ac,qcb->qab', left_inv, queries, precision=lax.Precision.HIGHEST)
    mixed_rows = jnp.einsum('qab,bd->qad', mixed_rows, right_inv, precision=lax.Precision.HIGHEST) * mean_total
    preconditioned = mixed_rows.reshape(QUERIES, FEATS).astype(jnp.bfloat16).reshape(N_DP, Q_DEV, FEATS)
    feature_blocks = features.reshape(N_DP, EX_DEV, FEATS)
    train_blocks = train_ids.reshape(N_DP, EX_DEV)
    query_blocks = query_ids.reshape(N_DP, Q_DEV)

    def score_tile(operands):
        query_part, query_tags, train_part, train_tags = operands
        scores = jnp.dot(query_part.astype(jnp.float32), train_part.astype(jnp.float32).T, precision=lax.Precision.HIGHEST)
        return jnp.where(query_tags[:, None] == train_tags[None, :], jnp.zeros_like(scores), scores)
    outputs = []
    for shift_step in range(STEPS):
        rolled = jnp.roll(preconditioned, shift_step, axis=0)
        rolled_ids = jnp.roll(query_blocks, shift_step, axis=0)
        score_tiles = lax.map(score_tile, (rolled, rolled_ids, feature_blocks, train_blocks))
        outputs.append(score_tiles.transpose(1, 0, 2).reshape(Q_DEV, TRAIN))
    return jnp.stack(outputs, 0)
```

```python
import jax
import jax.numpy as jnp
from jax import lax
from jax.experimental import pallas as pl
from jax.experimental.pallas import tpu as pltpu
from jax.sharding import PartitionSpec as P

K = 64
STEPS = 4
NX, NY, NZ, NF = 4, 8, 4, 4
N_DP = NX * NY * NZ
TRAIN = 131072
EX = 1024
COLS = 1024
PART = EX // NF
HALF = PART // 2
QD = 192
QROWS = QD // NF
DAMPING = 0.1

F32 = jnp.float32
BF16 = jnp.bfloat16


def dot_nt(a, b):
    return lax.dot_general(a, b, (((1,), (1,)), ((), ())), preferred_element_type=F32)


def dot_nn(a, b):
    return lax.dot_general(a, b, (((1,), (0,)), ((), ())), preferred_element_type=F32)


def identity(n):
    rows = lax.broadcasted_iota(jnp.int32, (n, n), 0)
    cols = lax.broadcasted_iota(jnp.int32, (n, n), 1)
    return jnp.where(rows == cols, 1.0, 0.0).astype(BF16)


def lower_lanes(rows):
    return lax.broadcasted_iota(jnp.int32, (rows, 2 * K), 1) < K


def fold(g):
    low = lower_lanes(K)
    h = jnp.where(low, g[0:64, 0:128], g[64:128, 0:128]) + jnp.where(
        low, g[128:192, 128:256], g[192:256, 128:256]
    )
    both = h + pltpu.roll(h, K, 1)
    return jnp.where(lower_lanes(32), both[0:32], both[32:64])


def split(v):
    high = v.astype(BF16)
    return high, (v - high.astype(F32)).astype(BF16)


def kernel(
    tg, qg, cnt, tid, qid, out,
    xr, xto, xt, xb, xbt, qall, prev, ids, prev_ids, m, w, st, acc, tcol,
    packed, rs_in, part, x_in, y_in, z_in, total, whole, inv, rsm, lsm,
    send, recv, local_sem,
):
    f = lax.axis_index("feat")
    i = lax.axis_index("dp")
    x = i % NX
    y = (i // NX) % NY
    zh = i // (NX * NY)

    def mate(d):
        if d == 0:
            return f
        if d == 1:
            return f + 1 - 2 * (f % 2)
        if d == 2:
            return (f + 2) % 4
        return 3 - f

    def on_x(d):
        return i - x + (x + d) % NX

    def on_y(d):
        return (zh * NY + (y + d) % NY) * NX + x

    def on_z(d):
        return (((zh + d) % NZ) * NY + y) * NX + x

    used = [0]

    def copy(src, dst, dp, ft, at=None):
        if at is None:
            at = used[0]
            used[0] += 1
        return pltpu.make_async_remote_copy(
            src_ref=src, dst_ref=dst, send_sem=send.at[at], recv_sem=recv.at[at],
            device_id=(dp, ft), device_id_type=pl.DeviceIdType.MESH,
        )

    barrier = pltpu.get_barrier_semaphore()
    partners = [(i, mate(d)) for d in (1, 2, 3)]
    partners += [(on_x(d), f) for d in range(1, NX)]
    partners += [(on_y(d), f) for d in range(1, NY)]
    partners += [(on_z(d), f) for d in range(1, NZ)]
    partners += [((i + NX) % N_DP, f), ((i + N_DP - NX) % N_DP, f)]
    for dp, ft in partners:
        pl.semaphore_signal(barrier, inc=1, device_id=(dp, ft), device_id_type=pl.DeviceIdType.MESH)
    pl.semaphore_wait(barrier, len(partners))

    sent = []

    def go(c):
        c.start()
        sent.append(c)
        return c

    regroup = {}
    for half in range(2):
        for d in (2, 3):
            rows = pl.ds(pl.multiple_of(mate(d) * PART + half * HALF, HALF), HALF)
            regroup[half, d] = go(copy(
                tg.at[rows, :], xr.at[d - 1, pl.ds(half * HALF, HALF), :], i, mate(d)))
    for half in range(2):
        rows = pl.ds(pl.multiple_of(mate(1) * PART + half * HALF, HALF), HALF)
        regroup[half, 1] = go(copy(
            tg.at[rows, :], xr.at[0, pl.ds(half * HALF, HALF), :], i, mate(1)))

    ids[0] = jnp.broadcast_to(qid[...], (8, 256))
    next_row = (i + NX) % N_DP
    to_prev = go(copy(qg, prev, next_row, f))
    to_prev_ids = go(copy(ids.at[0], prev_ids, next_row, f))
    right, left = on_x(1), on_x(NX - 1)

    def along(slot, src, src_ids, dp, at):
        return (copy(src, qall.at[slot, 0], dp, f, at), copy(src_ids, ids.at[slot], dp, f, at + 1))

    at_right = used[0]
    at_left = used[0] + 2
    at_relay_r = used[0] + 4
    at_relay_l = used[0] + 6
    used[0] += 8
    own_right = along(1, qg, ids.at[0], right, at_right)
    prev_right = along(1, prev, prev_ids, right, at_right)
    own_left = along(3, qg, ids.at[0], left, at_left)
    prev_left = along(3, prev, prev_ids, left, at_left)

    @pl.when(x < NX - 1)
    def _():
        for c in own_right:
            c.start()

    @pl.when(x == 0)
    def _():
        for c in own_left:
            c.start()

    core_a = [None] * STEPS
    z_a = [None] * STEPS
    core_b = [None] * STEPS
    for s in range(STEPS):
        src = qg if s == 0 else qall.at[s, 0]
        core_a[s] = copy(src, qall.at[s, 1], i, mate(1))
        z_a[s] = copy(src, qall.at[s, 2], i, mate(2))
        core_b[s] = copy(qall.at[s, 2], qall.at[s, 3], i, mate(1))
    go(core_a[0])

    qall[0, 0] = qg[...]

    def stages(n):
        c = {}
        c["rs"] = [copy(packed.at[n, pl.ds(pl.multiple_of(mate(d) * 8, 8), 8), :],
                        rs_in.at[n, d - 1], i, mate(d)) for d in (1, 2, 3)]
        c["x"] = [copy(part.at[n, 0], x_in.at[n, d - 1], on_x(d), f) for d in range(1, NX)]
        c["y"] = [copy(part.at[n, 1], y_in.at[n, d - 1], on_y(d), f) for d in range(1, NY)]
        c["z"] = [copy(part.at[n, 2], z_in.at[n, d - 1], on_z(d), f) for d in range(1, NZ)]
        c["ag"] = [copy(total.at[n, 0], total.at[n, d], i, mate(d)) for d in (1, 2, 3)]
        return c

    def start(cs):
        for c in cs:
            go(c)

    def arrived(cs):
        for c in cs:
            c.wait_recv()

    def add_up(first, ref, n, count):
        value = first
        for k in range(count):
            value = value + ref[n, k]
        return value

    def finish_rs(n, c):
        arrived(c["rs"])
        own = packed[n, pl.ds(pl.multiple_of(f * 8, 8), 8), :]
        part[n, 0] = add_up(own, rs_in, n, 3)

    def finish_x(n, c):
        arrived(c["x"])
        part[n, 1] = add_up(part[n, 0], x_in, n, NX - 1)

    def finish_y(n, c):
        arrived(c["y"])
        part[n, 2] = add_up(part[n, 1], y_in, n, NY - 1)

    def finish_z(n, c):
        arrived(c["z"])
        total[n, 0] = add_up(part[n, 2], z_in, n, NZ - 1)

    def finish_ag(n, c):
        arrived(c["ag"])
        for d in range(4):
            whole[n, pl.ds(pl.multiple_of(mate(d) * 8, 8), 8), :] = total[n, d]

    lane64 = lax.broadcasted_iota(jnp.int32, (K, 2 * K), 1) % K
    row64 = lax.broadcasted_iota(jnp.int32, (K, 2 * K), 0)
    lane1 = lax.broadcasted_iota(jnp.int32, (1, 2 * K), 1) % K

    def invert(n):
        s = whole[n]
        r = pltpu.roll(s, K, 1)
        low = lower_lanes(32)
        full = jnp.concatenate([jnp.where(low, s, r), jnp.where(low, r, s)], axis=0)
        diag = lane64 == row64
        trace = jnp.sum(jnp.where(diag, full, 0.0)) * 0.5
        mean_total = trace / TRAIN
        inv[n] = full / TRAIN + jnp.where(diag, DAMPING * mean_total / K, 0.0)

        def step(k, carry):
            a = inv[n]
            row = inv[n, pl.ds(k, 1), :]
            col = jnp.sum(jnp.where(lane64 == k, a, 0.0), axis=1, keepdims=True) * 0.5
            pivot = jnp.sum(jnp.where(lane1 == k, row, 0.0), axis=1, keepdims=True) * 0.5
            scaled = jnp.where(lane1 == k, 1.0, row) * (1.0 / pivot)
            updated = jnp.where(lane64 == k, 0.0, a) - col * scaled
            inv[n] = jnp.where(row64 == k, scaled, updated)
            return carry

        lax.fori_loop(0, K, step, 0)
        return mean_total

    rcp = 1.0 / cnt[...].astype(F32)
    eye = identity(128)
    for k in range(COLS // 128):
        t = dot_nt(eye, tg[:, k * 128:(k + 1) * 128])
        xto[k * 128:(k + 1) * 128, :] = (t * rcp).astype(BF16)
    g = jnp.zeros((256, 256), F32)
    for k in range(COLS // 256):
        rows = xto[k * 256:(k + 1) * 256, :]
        g = g + dot_nt(rows, rows)
    packed[0] = fold(g)
    c0 = stages(0)
    start(c0["rs"])
    finish_rs(0, c0)
    start(c0["x"])
    finish_x(0, c0)

    to_prev.wait_recv()
    to_prev_ids.wait_recv()

    @pl.when(x == NX - 1)
    def _():
        for c in prev_right:
            c.start()

    @pl.when(x > 0)
    def _():
        for c in prev_left:
            c.start()

    start(c0["y"])
    finish_y(0, c0)
    start(c0["z"])
    finish_z(0, c0)
    start(c0["ag"])
    finish_ag(0, c0)

    invert(0)
    low = lower_lanes(K)
    full = inv[0]
    hi, rest = split(full)
    rest32 = full - hi.astype(F32)
    mid = rest32.astype(BF16)
    tiny = (rest32 - mid.astype(F32)).astype(BF16)
    for n, term in enumerate((hi, mid, tiny)):
        zero = jnp.zeros_like(term)
        rsm[n * 128:n * 128 + 64, :] = jnp.where(low, term, zero)
        rsm[n * 128 + 64:n * 128 + 128, :] = jnp.where(low, zero, term)

    own_lanes = pl.ds(pl.multiple_of(f * PART, PART), PART)
    rcp_part = 1.0 / cnt[:, own_lanes].astype(F32)

    def transpose_half(half):
        scale = rcp_part[:, half * HALF:(half + 1) * HALF]
        for d in range(4):
            base = mate(d) * COLS
            for k in range(COLS // 128):
                cols = slice(k * 128, (k + 1) * 128)
                if d == 0:
                    rows = pl.ds(pl.multiple_of(f * PART + half * HALF, HALF), HALF)
                    block = tg[rows, cols]
                else:
                    block = xr[d - 1, half * HALF:(half + 1) * HALF, cols]
                t = (dot_nt(eye, block) * scale).astype(BF16).astype(F32)
                xt[half, pl.ds(pl.multiple_of(base + k * 128, 128), 128), :] = t

    arrived([regroup[0, d] for d in (1, 2, 3)])
    transpose_half(0)

    for c in own_right:
        c.wait_recv()
    for c in own_left:
        c.wait_recv()
    relay_r = along(2, qall.at[1, 0], ids.at[1], right, at_relay_r)
    relay_l = along(2, qall.at[3, 0], ids.at[3], left, at_relay_l)

    relays = (x == 1) | (x == 2)

    @pl.when(relays)
    def _():
        for c in relay_r + relay_l:
            c.start()

    go(core_a[1])
    go(core_a[3])

    arrived([regroup[1, d] for d in (1, 2, 3)])
    go(z_a[0])
    transpose_half(1)

    def regather(b, carry):
        for half in range(2):
            rows = xt[half, pl.ds(b, K, stride=K), :].astype(BF16)
            xb[pl.ds(pl.multiple_of(b * K, K), K), half * HALF:(half + 1) * HALF] = rows
        return carry

    lax.fori_loop(0, K, regather, 0, unroll=4)

    acc_g = jnp.zeros((256, 256), F32)

    def add_gram(k, total_g):
        rows = xb[pl.ds(pl.multiple_of(k * 256, 256), 256), :]
        return total_g + dot_nt(rows, rows)

    acc_g = lax.fori_loop(0, 16, add_gram, acc_g)
    packed[1] = fold(acc_g)
    c1 = stages(1)
    start(c1["rs"])
    go(z_a[1])
    go(z_a[3])
    finish_rs(1, c1)
    start(c1["x"])

    eye256 = identity(256)

    def put_back(k, carry):
        at = pl.multiple_of(k * 256, 256)
        xbt[:, pl.ds(at, 256)] = dot_nt(eye256, xb[pl.ds(at, 256), :]).astype(BF16)
        return carry

    lax.fori_loop(0, 16, put_back, 0)
    finish_x(1, c1)
    start(c1["y"])
    tcol[...] = jnp.broadcast_to(tid[:, own_lanes], (128, PART)).T
    finish_y(1, c1)
    start(c1["z"])

    @pl.when(x >= 2)
    def _():
        for c in relay_r:
            c.wait_recv()

    @pl.when(x < 2)
    def _():
        for c in relay_l:
            c.wait_recv()

    go(z_a[2])
    go(core_a[2])
    finish_z(1, c1)
    start(c1["ag"])
    finish_ag(1, c1)
    mean_total = invert(1)
    full = inv[1] * mean_total
    hi, lo = split(full)
    lsm[0:64, :] = hi
    lsm[64:128, :] = jnp.where(low, lo, jnp.zeros_like(lo))

    def right_product(s, d):
        base = mate(d) * COLS

        def step(k, carry):
            cols = pl.ds(pl.multiple_of(k * 128, 128), 128)
            t = dot_nt(rsm[...], qall[s, d, :, cols])
            t = t[0:128] + (t[128:256] + t[256:384])
            rows = pl.ds(pl.multiple_of(base + k * 128, 128), 128)
            m[0, rows, :] = t[:, 0:128]
            m[1, rows, 0:64] = t[:, 128:192]
            return carry

        lax.fori_loop(0, COLS // 128, step, 0)

    def regroup_queries(s):
        def step(b, carry):
            at = pl.multiple_of(b * 2 * K, 2 * K)
            for j, lanes in enumerate((128, 64)):
                hi, lo = split(m[j, pl.ds(b, K, stride=K), :][:, 0:lanes])
                w[s, pl.ds(at, K), j * 128:j * 128 + lanes] = hi
                w[s, pl.ds(at + K, K), j * 128:j * 128 + lanes] = lo
            return carry

        lax.fori_loop(0, K, step, 0, unroll=2)

    def scores(s):
        acc[...] = jnp.zeros_like(acc)

        def step(g, carry):
            pieces = []
            for j in range(4):
                at = pl.multiple_of(g * 512 + j * 128, 128)
                t = dot_nn(lsm[...], w[s, pl.ds(at, 128), :])
                pieces.append((t[0:64] + t[64:128]).astype(BF16))
            at = pl.multiple_of(g * 256, 256)
            acc[...] += dot_nn(xbt[:, pl.ds(at, 256)], jnp.concatenate(pieces, axis=0))
            return carry

        lax.fori_loop(0, 16, step, 0)
        same = tcol[:, 0:1] == ids[s, 0:1, 0:QD]
        st[s] = jnp.where(same, 0.0, acc[...]).T

    results = []
    for s in (0, 1, 3, 2):
        core_a[s].wait_recv()
        z_a[s].wait_recv()
        go(core_b[s])
        right_product(s, 0)
        right_product(s, 1)
        right_product(s, 2)
        core_b[s].wait_recv()
        right_product(s, 3)
        regroup_queries(s)
        scores(s)
        for d in (2, 3, 1):
            results.append(go(copy(
                st.at[s, pl.ds(pl.multiple_of(mate(d) * QROWS, 8), QROWS), :],
                out.at[s, :, own_lanes], i, mate(d))))
        out[s, :, own_lanes] = st[s, pl.ds(pl.multiple_of(f * QROWS, 8), QROWS), :]

    for c in results:
        c.wait_recv()
    for c in sent:
        c.wait_send()
    for c in own_right + own_left:
        c.wait_send()

    @pl.when(relays)
    def _():
        for c in relay_r + relay_l:
            c.wait_send()


N_SEM = 80


def on_device(train_grads, token_counts, train_ids, query_grads, query_ids):
    cnt = token_counts.reshape(1, EX)
    tid = train_ids.reshape(1, EX)
    qid = jnp.pad(query_ids, (0, 256 - QD)).reshape(1, 256)
    vmem = pltpu.VMEM
    scratch = [
        vmem((3, PART, COLS), BF16),
        vmem((COLS, EX), BF16),
        vmem((2, K * K, HALF), F32),
        vmem((K * K, PART), BF16),
        vmem((PART, K * K), BF16),
        vmem((STEPS, NF, QD, COLS), BF16),
        vmem((QD, COLS), BF16),
        vmem((STEPS, 8, 256), jnp.int32),
        vmem((8, 256), jnp.int32),
        vmem((2, K * K, 128), F32),
        vmem((STEPS, 2 * K * K, QD), BF16),
        vmem((STEPS, QD, PART), F32),
        vmem((PART, QD), F32),
        vmem((PART, 128), jnp.int32),
        vmem((2, 32, 128), F32),
        vmem((2, 3, 8, 128), F32),
        vmem((2, 3, 8, 128), F32),
        vmem((2, NX - 1, 8, 128), F32),
        vmem((2, NY - 1, 8, 128), F32),
        vmem((2, NZ - 1, 8, 128), F32),
        vmem((2, 4, 8, 128), F32),
        vmem((2, 32, 128), F32),
        vmem((2, K, 2 * K), F32),
        vmem((384, 128), BF16),
        vmem((128, 128), BF16),
        pltpu.SemaphoreType.DMA((N_SEM,)),
        pltpu.SemaphoreType.DMA((N_SEM,)),
        pltpu.SemaphoreType.DMA,
    ]
    spec = pl.BlockSpec(memory_space=pltpu.VMEM)
    return pl.pallas_call(
        kernel,
        out_shape=jax.ShapeDtypeStruct((STEPS, QROWS, EX), F32),
        in_specs=[spec] * 5,
        out_specs=spec,
        scratch_shapes=scratch,
        compiler_params=pltpu.CompilerParams(
            collective_id=0, has_side_effects=True, vmem_limit_bytes=58 * 1024 * 1024
        ),
        cost_estimate=pl.CostEstimate(flops=4_000_000_000, bytes_accessed=8_000_000, transcendentals=0),
    )(train_grads, query_grads, cnt, tid, qid)


def solution(mesh):
    in_specs = (P("dp", "feat"), P("dp"), P("dp"), P("dp", "feat"), P("dp"))
    out_specs = P(None, "feat", "dp")
    return jax.shard_map(
        on_device, mesh=mesh, in_specs=in_specs, out_specs=out_specs, check_vma=False
    )
```

```python
import jax
import jax.numpy as jnp
from jax import lax
from jax.experimental import pallas as pl
from jax.experimental.pallas import tpu as pltpu
from jax.sharding import PartitionSpec as P

K = 64
PITCH = 72
STEPS = 4
NX, NY, NZ, NF = 4, 8, 4, 4
N_DP = NX * NY * NZ
TRAIN = 131072
EX = 1024
COLS = 1024
PART = EX // NF
HALF = PART // 2
QD = 192
QROWS = QD // NF
DAMPING = 0.1

F32 = jnp.float32
BF16 = jnp.bfloat16


def dot_nt(a, b):
    return lax.dot_general(a, b, (((1,), (1,)), ((), ())), preferred_element_type=F32)


def dot_nn(a, b):
    return lax.dot_general(a, b, (((1,), (0,)), ((), ())), preferred_element_type=F32)


def identity(n):
    rows = lax.broadcasted_iota(jnp.int32, (n, n), 0)
    cols = lax.broadcasted_iota(jnp.int32, (n, n), 1)
    return jnp.where(rows == cols, 1.0, 0.0).astype(BF16)


def lower_lanes(rows):
    return lax.broadcasted_iota(jnp.int32, (rows, 2 * K), 1) < K


def fold(g):
    low = lower_lanes(K)
    h = jnp.where(low, g[0:64, 0:128], g[64:128, 0:128]) + jnp.where(
        low, g[128:192, 128:256], g[192:256, 128:256]
    )
    both = h + pltpu.roll(h, K, 1)
    return jnp.where(lower_lanes(32), both[0:32], both[32:64])


def split(v):
    high = v.astype(BF16)
    return high, (v - high.astype(F32)).astype(BF16)


def kernel(
    tg, qg, cnt, tid, qid, out,
    xr, xto, xt, xb, xbt, qall, prev, hop1, hop2, ids, prev_ids, hop_ids, m, w, st, p, tcol,
    packed, c_in, part, x_in, y_in, z_in, total, other, whole, inv, rsm, lsm,
    send, recv,
):
    f = lax.axis_index("feat")
    i = lax.axis_index("dp")
    x = i % NX
    y = (i // NX) % NY
    zh = i // (NX * NY)
    core = f % 2
    z = 2 * zh + f // 2

    def mate(d):
        if d == 0:
            return f
        if d == 1:
            return f + 1 - 2 * core
        if d == 2:
            return (f + 2) % 4
        return 3 - f

    def on_x(d):
        return i - x + (x + d) % NX, f

    def on_y(d):
        return (zh * NY + (y + d) % NY) * NX + x, f

    def on_z(d):
        there = (z + d) % (2 * NZ)
        return ((there // 2) * NY + y) * NX + x, (there % 2) * 2 + core

    def in_group(d):
        return i, mate(d)

    used = [0]

    def reserve(n=1):
        used[0] += n
        return used[0] - n

    def copy(src, dst, device, at=None, recv_at=None):
        at = reserve() if at is None else at
        recv_at = at if recv_at is None else recv_at
        return pltpu.make_async_remote_copy(
            src_ref=src, dst_ref=dst, send_sem=send.at[at], recv_sem=recv.at[recv_at],
            device_id=device, device_id_type=pl.DeviceIdType.MESH,
        )

    barrier = pltpu.get_barrier_semaphore()
    partners = [in_group(1), in_group(3)]
    partners += [on_x(d) for d in range(1, NX)]
    partners += [on_y(d) for d in range(1, NY)]
    partners += [on_z(d) for d in range(1, 2 * NZ)]
    for device in partners:
        pl.semaphore_signal(barrier, inc=1, device_id=device, device_id_type=pl.DeviceIdType.MESH)
    pl.semaphore_wait(barrier, len(partners))

    sent = []

    def go(c):
        c.start()
        sent.append((None, c))
        return c

    def go_if(cond, cs):
        @pl.when(cond)
        def _():
            for c in cs:
                c.start()

        sent.extend((cond, c) for c in cs)

    def arrived(cs):
        for c in cs:
            c.wait_recv()

    def arrived_if(cond, cs):
        @pl.when(cond)
        def _():
            for c in cs:
                c.wait_recv()

    qall[0, 0] = qg[...]
    ids[0] = jnp.zeros((8, 256), jnp.int32)
    ids[0, :, 0:QD] = jnp.broadcast_to(qid[...], (8, QD))
    core_a = [copy(qall.at[s, 0], qall.at[s, 1], in_group(1)) for s in range(STEPS)]
    core_b = [copy(qall.at[s, 2], qall.at[s, 3], in_group(1)) for s in range(STEPS)]
    z_a = {s: copy(qall.at[s, 0], qall.at[s, 2], in_group(2)) for s in (0, 2)}

    def regroup(half, d):
        rows = pl.ds(pl.multiple_of(mate(d) * PART + half * HALF, HALF), HALF)
        return copy(tg.at[rows, :], xr.at[d - 1, pl.ds(half * HALF, HALF), :], in_group(d))

    regrouped = {(half, d): regroup(half, d) for half in range(2) for d in (2, 3, 1)}

    to_next = [copy(qall.at[0, 2 * n], prev.at[n], on_y(1)) for n in range(2)]
    at_prev_ids = reserve()
    to_next_ids = copy(ids.at[0], prev_ids, on_y(1), None, at_prev_ids)
    wrap_ids_1 = copy(ids.at[0], hop_ids, on_z(2))
    wrap_ids_2 = copy(hop_ids, prev_ids, on_y(1), None, at_prev_ids)
    wrap_1, wrap_2, wrap_3, wrap_in = [], [], [], []
    for n in range(2):
        got = reserve()
        wrap_1.append([
            copy(qall.at[0, 2 * n, :, pl.ds((d - 1) * 128, 128)], hop1.at[n], on_y(d), None, got)
            for d in range(1, NY)])
        wrap_2.append(copy(hop1.at[n], hop2.at[n], on_z(2)))
        first = reserve(NY)
        at = reserve()
        to_first = (zh * NY * NX + x, f)
        lanes = pl.ds(pl.multiple_of(y * 128, 128), 128)
        wrap_3.append(copy(hop2.at[n], prev.at[n, :, lanes], to_first, at, first + y))
        wrap_in.append([
            copy(hop2.at[n], prev.at[n, :, pl.ds(j * 128, 128)], to_first, at, first + j)
            for j in range(1, NY)])

    def send_next(n):
        go_if(y < NY - 1, [to_next[n]])
        go_if(y == NY - 1, wrap_1[n])

        @pl.when(y == NY - 1)
        def _():
            hop1[n] = qall[0, 2 * n, :, (NY - 1) * 128:NY * 128]

    def send_wrap_2(n):
        @pl.when(y < NY - 1)
        def _():
            wrap_1[n][0].wait_recv()

        go(wrap_2[n])

    def send_wrap_3(n):
        wrap_2[n].wait_recv()
        go_if(y > 0, [wrap_3[n]])

        @pl.when(y == 0)
        def _():
            prev[n, :, 0:128] = hop2[n]

    def wait_prev(n):
        arrived_if(y > 0, [to_next[n]])
        arrived_if(y == 0, wrap_in[n])

    right, left = on_x(1), on_x(NX - 1)
    at_right, at_left, at_relay = reserve(2), reserve(2), reserve(2)
    at_ids = reserve(4)
    own_right = [copy(qall.at[0, 2 * n], qall.at[1, 2 * n], right, at_right + n) for n in range(2)]
    prev_right = [copy(prev.at[n], qall.at[1, 2 * n], right, at_right + n) for n in range(2)]
    own_left = [copy(qall.at[0, 2 * n], qall.at[3, 2 * n], left, at_left + n) for n in range(2)]
    prev_left = [copy(prev.at[n], qall.at[3, 2 * n], left, at_left + n) for n in range(2)]
    own_right_ids = copy(ids.at[0], ids.at[1], right, at_ids)
    prev_right_ids = copy(prev_ids, ids.at[1], right, at_ids)
    own_left_ids = copy(ids.at[0], ids.at[3], left, at_ids + 1)
    prev_left_ids = copy(prev_ids, ids.at[3], left, at_ids + 1)
    relay_r = [copy(qall.at[1, 0], qall.at[2, 0], right, at_relay),
               copy(ids.at[1], ids.at[2], right, at_ids + 2)]
    relay_l = [copy(qall.at[3, 0], qall.at[2, 0], left, at_relay + 1),
               copy(ids.at[3], ids.at[2], left, at_ids + 3)]
    relays = (x == 1) | (x == 2)

    def send_own(n):
        more = n == 0
        go_if(x < NX - 1, [own_right[n]] + [own_right_ids] * more)
        go_if(x == 0, [own_left[n]] + [own_left_ids] * more)

    def send_prev(n):
        more = n == 0
        go_if(x == NX - 1, [prev_right[n]] + [prev_right_ids] * more)
        go_if(x > 0, [prev_left[n]] + [prev_left_ids] * more)

    class Sum:
        def __init__(self, n):
            self.n = n
            self.mine = pl.ds(pl.multiple_of(core * 16, 16), 16)
            self.theirs = pl.ds(pl.multiple_of((1 - core) * 16, 16), 16)
            self.c = copy(packed.at[n, self.theirs, :], c_in.at[n], in_group(1))
            self.x = [copy(part.at[n, 0], x_in.at[n, d - 1], on_x(d)) for d in range(1, NX)]
            self.y = [copy(part.at[n, 1], y_in.at[n, d - 1], on_y(d)) for d in range(1, NY)]
            self.z = [copy(part.at[n, 2], z_in.at[n, d - 1], on_z(d)) for d in range(1, 2 * NZ)]
            self.back = copy(total.at[n], other.at[n], in_group(1))

        def send(self, cs):
            for c in cs:
                go(c)

        def collect(self, cs, first, ref):
            arrived(cs)
            value = first
            for k in range(len(cs)):
                value = value + ref[self.n, k]
            return value

        def start(self):
            go(self.c)

        def start_x(self):
            self.c.wait_recv()
            part[self.n, 0] = packed[self.n, self.mine, :] + c_in[self.n]
            self.send(self.x)

        def start_y(self):
            part[self.n, 1] = self.collect(self.x, part[self.n, 0], x_in)
            self.send(self.y)

        def start_z(self):
            part[self.n, 2] = self.collect(self.y, part[self.n, 1], y_in)
            self.send(self.z)

        def start_back(self):
            total[self.n] = self.collect(self.z, part[self.n, 2], z_in)
            go(self.back)

        def finish(self):
            self.back.wait_recv()
            whole[self.n, self.mine, :] = total[self.n]
            whole[self.n, self.theirs, :] = other[self.n]

    tile = (8, 8, 128)
    lane64 = lax.broadcasted_iota(jnp.int32, (K, 2 * K), 1) % K
    row64 = lax.broadcasted_iota(jnp.int32, (K, 2 * K), 0)
    lane8 = lax.broadcasted_iota(jnp.int32, (8, 2 * K), 1) % K
    row_of = row64.reshape(tile)
    low = lower_lanes(K)

    def invert(n):
        s = whole[n]
        r = pltpu.roll(s, K, 1)
        low32 = lower_lanes(32)
        full = jnp.concatenate([jnp.where(low32, s, r), jnp.where(low32, r, s)], axis=0)
        diag = lane64 == row64
        trace = jnp.sum(jnp.where(diag, full, 0.0)) * 0.5
        mean_total = trace / TRAIN
        inv[n] = full / TRAIN + jnp.where(diag, DAMPING * mean_total / K, 0.0)
        for k in range(0, K, 4):
            a = inv[n]
            spots = [jnp.full((8, 128), k + j, jnp.int32) for j in range(4)]
            rows = [jnp.broadcast_to(inv[n, k + j:k + j + 1, :], (8, 128)) for j in range(4)]
            e = [[jnp.take_along_axis(rows[j], spots[t], axis=1) for t in range(4)] for j in range(4)]
            cols = [
                jnp.take_along_axis(a, jnp.full((K, 128), k + j, jnp.int32), axis=1).reshape(tile)
                for j in range(4)]
            for t in range(4):
                pivot = 1.0 / e[t][t]
                here = lane8 == k + t
                rows[t] = jnp.where(here, 1.0, rows[t]) * pivot
                scaled = [e[t][v] * pivot for v in range(4)]
                for j in range(4):
                    if j != t:
                        rows[j] = jnp.where(here, 0.0, rows[j]) - e[j][t] * rows[t]
                        for v in range(t + 1, 4):
                            e[j][v] = e[j][v] - e[j][t] * scaled[v]
                for v in range(t + 1, 4):
                    e[t][v] = scaled[v]
            inside = (lane8 >= k) & (lane8 < k + 4)
            u = jnp.where(inside[None], 0.0, a.reshape(tile))
            for j in range(4):
                u = u - cols[j] * rows[j][None]
            for j in range(4):
                u = jnp.where(row_of == k + j, rows[j][None], u)
            inv[n] = u.reshape(K, 2 * K)
        return mean_total

    eye = identity(128)
    own_lanes = pl.ds(pl.multiple_of(f * PART, PART), PART)
    rcp_part = 1.0 / cnt[:, own_lanes].astype(F32)

    def transpose(half, d):
        scale = rcp_part[:, half * HALF:(half + 1) * HALF]
        base = mate(d) * (COLS // K * PITCH)
        for k in range(COLS // 128):
            cols = slice(k * 128, (k + 1) * 128)
            if d == 0:
                rows = pl.ds(pl.multiple_of(f * PART + half * HALF, HALF), HALF)
                block = tg[rows, cols]
            else:
                block = xr[d - 1, half * HALF:(half + 1) * HALF, cols]
            t = (dot_nt(eye, block) * scale).astype(BF16).astype(F32)
            for j in range(2):
                xt[half, pl.ds(pl.multiple_of(base + (2 * k + j) * PITCH, 8), K), :] = t[j * K:(j + 1) * K]

    def right_product(s, d):
        base = mate(d) * (COLS // K * PITCH)
        for k in range(COLS // 128):
            t = dot_nt(rsm[...], qall[s, d, :, k * 128:(k + 1) * 128])
            t = t[0:128] + (t[128:256] + t[256:384])
            for j in range(2):
                rows = pl.ds(pl.multiple_of(base + (2 * k + j) * PITCH, 8), K)
                m[0, rows, :] = t[j * K:(j + 1) * K, 0:128]
                m[1, rows, 0:64] = t[j * K:(j + 1) * K, 128:192]

    def prepare(s):
        for d in range(4):
            right_product(s, d)

        def step(b, carry):
            at = pl.multiple_of(b * 2 * K, 2 * K)
            for j, lanes in enumerate((128, 64)):
                hi, lo = split(m[j, pl.ds(b, K, stride=PITCH), :][:, 0:lanes])
                w[s, pl.ds(at, K), j * 128:j * 128 + lanes] = hi
                w[s, pl.ds(at + K, K), j * 128:j * 128 + lanes] = lo
            return carry

        lax.fori_loop(0, K, step, 0, unroll=8)

    def scores(s):
        def step(b, carry):
            at = pl.multiple_of(b * 128, 128)
            t = dot_nn(lsm[...], w[s, pl.ds(at, 128), :])
            p[pl.ds(pl.multiple_of(b * K, K), K), :] = (t[0:64] + t[64:128]).astype(BF16)
            return carry

        lax.fori_loop(0, K, step, 0, unroll=32)
        value = dot_nn(xbt[...], p[...])
        same = tcol[:, 0:1] == ids[s, 0:1, 0:QD]
        st[s] = jnp.where(same, 0.0, value).T

    results = []

    def hand_out(s):
        for d in (2, 3, 1):
            results.append(go(copy(
                st.at[s, pl.ds(pl.multiple_of(mate(d) * QROWS, 8), QROWS), :],
                out.at[s, :, own_lanes], in_group(d))))
        out[s, :, own_lanes] = st[s, pl.ds(pl.multiple_of(f * QROWS, 8), QROWS), :]

    go(z_a[0])
    go(regrouped[0, 2])
    go(regrouped[0, 3])
    go(core_a[0])
    go(regrouped[0, 1])
    go(regrouped[1, 1])
    send_next(0)
    go_if(y < NY - 1, [to_next_ids])
    go_if(y == NY - 1, [wrap_ids_1])

    rcp = 1.0 / cnt[...].astype(F32)
    for k in range(COLS // 128):
        t = dot_nt(eye, tg[:, k * 128:(k + 1) * 128])
        xto[k * 128:(k + 1) * 128, :] = (t * rcp).astype(BF16)
    g = jnp.zeros((256, 256), F32)
    for k in range(COLS // 256):
        rows = xto[k * 256:(k + 1) * 256, :]
        g = g + dot_nt(rows, rows)
    packed[0] = fold(g)
    sum0 = Sum(0)
    sum0.start()
    sum0.start_x()
    send_own(0)
    send_wrap_2(0)
    transpose(0, 0)
    transpose(1, 0)
    tcol[...] = jnp.broadcast_to(tid[:, own_lanes], (128, PART)).T
    arrived([regrouped[0, 1], regrouped[1, 1]])
    transpose(0, 1)
    transpose(1, 1)
    send_wrap_3(0)
    sum0.start_y()
    z_a[0].wait_recv()
    send_next(1)
    send_own(1)
    go(core_b[0])
    arrived_if(y == NY - 1, [wrap_ids_1])
    go_if(y == NY - 1, [wrap_ids_2])
    wait_prev(0)
    to_next_ids.wait_recv()
    send_prev(0)
    sum0.start_z()
    go(regrouped[1, 2])
    go(regrouped[1, 3])
    send_wrap_2(1)
    arrived([own_right[0], own_left[0], own_right_ids, own_left_ids])
    go_if(relays, relay_r + relay_l)
    go(core_a[1])
    go(core_a[3])
    send_wrap_3(1)
    wait_prev(1)
    send_prev(1)
    arrived([regrouped[0, 2], regrouped[0, 3]])
    transpose(0, 2)
    transpose(0, 3)
    sum0.start_back()
    sum0.finish()
    invert(0)
    full = inv[0]
    hi = full.astype(BF16)
    rest = full - hi.astype(F32)
    mid, tiny = split(rest)
    zero = jnp.zeros_like(hi)
    for n, term in enumerate((hi, mid, tiny)):
        rsm[n * 128:n * 128 + 64, :] = jnp.where(low, term, zero)
        rsm[n * 128 + 64:n * 128 + 128, :] = jnp.where(low, zero, term)
    arrived([core_a[0], core_b[0]])
    prepare(0)
    arrived([own_right[1], own_left[1]])
    go(core_b[1])
    go(core_b[3])

    arrived([regrouped[1, 2], regrouped[1, 3]])
    transpose(1, 2)
    transpose(1, 3)

    def regather(b, carry):
        for half in range(2):
            rows = xt[half, pl.ds(b, K, stride=PITCH), :].astype(BF16)
            xb[pl.ds(pl.multiple_of(b * K, K), K), half * HALF:(half + 1) * HALF] = rows
        return carry

    lax.fori_loop(0, K, regather, 0, unroll=8)

    def add_gram(k, total_g):
        rows = xb[pl.ds(pl.multiple_of(k * 256, 256), 256), :]
        return total_g + dot_nt(rows, rows)

    packed[1] = fold(lax.fori_loop(0, 16, add_gram, jnp.zeros((256, 256), F32), unroll=4))
    sum1 = Sum(1)
    sum1.start()
    sum1.start_x()
    eye256 = identity(256)

    def put_back(k, carry):
        at = pl.multiple_of(k * 256, 256)
        xbt[:, pl.ds(at, 256)] = dot_nt(eye256, xb[pl.ds(at, 256), :]).astype(BF16)
        return carry

    lax.fori_loop(0, 16, put_back, 0, unroll=4)
    arrived_if(x >= 2, relay_r)
    arrived_if(x < 2, relay_l)
    go(z_a[2])
    go(core_a[2])
    sum1.start_y()
    arrived([core_a[1], core_b[1]])
    prepare(1)
    sum1.start_z()
    arrived([core_a[3], core_b[3]])
    prepare(3)
    sum1.start_back()
    sum1.finish()
    mean_total = invert(1)
    hi, lo = split(inv[1] * mean_total)
    lsm[0:64, :] = hi
    lsm[64:128, :] = jnp.where(low, lo, jnp.zeros_like(lo))

    z_a[2].wait_recv()
    go(core_b[2])
    scores(0)
    hand_out(0)
    scores(1)
    hand_out(1)
    scores(3)
    hand_out(3)
    arrived([core_a[2], core_b[2]])
    prepare(2)
    scores(2)
    hand_out(2)

    assert used[0] <= N_SEM, used
    arrived(results)
    for cond, c in sent:
        if cond is None:
            c.wait_send()
    for cond, c in sent:
        if cond is not None:
            pl.when(cond)(c.wait_send)


N_SEM = 136


def on_device(train_grads, token_counts, train_ids, query_grads, query_ids):
    cnt = token_counts.reshape(1, EX)
    tid = train_ids.reshape(1, EX)
    qid = query_ids.reshape(1, QD)
    vmem = pltpu.VMEM
    scratch = [
        vmem((3, PART, COLS), BF16),
        vmem((COLS, EX), BF16),
        vmem((2, K * PITCH, HALF), F32),
        vmem((K * K, PART), BF16),
        vmem((PART, K * K), BF16),
        vmem((STEPS, NF, QD, COLS), BF16),
        vmem((2, QD, COLS), BF16),
        vmem((2, QD, 128), BF16),
        vmem((2, QD, 128), BF16),
        vmem((STEPS, 8, 256), jnp.int32),
        vmem((8, 256), jnp.int32),
        vmem((8, 256), jnp.int32),
        vmem((2, K * PITCH, 128), F32),
        vmem((STEPS, 2 * K * K, QD), BF16),
        vmem((STEPS, QD, PART), F32),
        vmem((K * K, QD), BF16),
        vmem((PART, 128), jnp.int32),
        vmem((2, 32, 128), F32),
        vmem((2, 16, 128), F32),
        vmem((2, 3, 16, 128), F32),
        vmem((2, NX - 1, 16, 128), F32),
        vmem((2, NY - 1, 16, 128), F32),
        vmem((2, 2 * NZ - 1, 16, 128), F32),
        vmem((2, 16, 128), F32),
        vmem((2, 16, 128), F32),
        vmem((2, 32, 128), F32),
        vmem((2, K, 2 * K), F32),
        vmem((384, 128), BF16),
        vmem((128, 128), BF16),
        pltpu.SemaphoreType.DMA((N_SEM,)),
        pltpu.SemaphoreType.DMA((N_SEM,)),
    ]
    spec = pl.BlockSpec(memory_space=pltpu.VMEM)
    return pl.pallas_call(
        kernel,
        out_shape=jax.ShapeDtypeStruct((STEPS, QROWS, EX), F32),
        in_specs=[spec] * 5,
        out_specs=spec,
        scratch_shapes=scratch,
        compiler_params=pltpu.CompilerParams(
            collective_id=0, has_side_effects=True, vmem_limit_bytes=58 * 1024 * 1024
        ),
        cost_estimate=pl.CostEstimate(flops=4_000_000_000, bytes_accessed=8_000_000, transcendentals=0),
    )(train_grads, query_grads, cnt, tid, qid)


def solution(mesh):
    in_specs = (P("dp", "feat"), P("dp"), P("dp"), P("dp", "feat"), P("dp"))
    out_specs = P(None, "feat", "dp")
    return jax.shard_map(
        on_device, mesh=mesh, in_specs=in_specs, out_specs=out_specs, check_vma=False
    )
```

```python
import jax
import jax.numpy as jnp
from jax import lax
from jax.experimental import pallas as pl
from jax.experimental.pallas import tpu as pltpu
from jax.sharding import PartitionSpec as P

K = 64
PITCH = 72
STEPS = 4
NX, NY, NZ, NF = 4, 8, 4, 4
N_DP = NX * NY * NZ
TRAIN = 131072
EX = 1024
COLS = 1024
PART = EX // NF
HALF = PART // 2
QD = 192
QROWS = QD // NF
DAMPING = 0.1

F32 = jnp.float32
BF16 = jnp.bfloat16


def dot_nt(a, b):
    return lax.dot_general(a, b, (((1,), (1,)), ((), ())), preferred_element_type=F32)


def dot_nn(a, b):
    return lax.dot_general(a, b, (((1,), (0,)), ((), ())), preferred_element_type=F32)


def identity(n):
    rows = lax.broadcasted_iota(jnp.int32, (n, n), 0)
    cols = lax.broadcasted_iota(jnp.int32, (n, n), 1)
    return jnp.where(rows == cols, 1.0, 0.0).astype(BF16)


def lower_lanes(rows):
    return lax.broadcasted_iota(jnp.int32, (rows, 2 * K), 1) < K


def fold(g):
    low = lower_lanes(K)
    h = jnp.where(low, g[0:64, 0:128], g[64:128, 0:128]) + jnp.where(
        low, g[128:192, 128:256], g[192:256, 128:256]
    )
    both = h + pltpu.roll(h, K, 1)
    return jnp.where(lower_lanes(32), both[0:32], both[32:64])


def split(v):
    high = v.astype(BF16)
    return high, (v - high.astype(F32)).astype(BF16)


def kernel(
    tg, qg, cnt, tid, qid, out,
    xr, xto, xt, xb, xbt, qall, prev, hop1, hop2, ids, prev_ids, hop_ids, m, w, st, p, tcol,
    packed, c_in, part, x_in, y_in, z_in, total, other, whole, inv, rsm, lsm,
    send, recv,
):
    f = lax.axis_index("feat")
    i = lax.axis_index("dp")
    x = i % NX
    y = (i // NX) % NY
    zh = i // (NX * NY)
    core = f % 2
    z = 2 * zh + f // 2

    def mate(d):
        if d == 0:
            return f
        if d == 1:
            return f + 1 - 2 * core
        if d == 2:
            return (f + 2) % 4
        return 3 - f

    def on_x(d):
        return i - x + (x + d) % NX, f

    def on_y(d):
        return (zh * NY + (y + d) % NY) * NX + x, f

    def on_z(d):
        there = (z + d) % (2 * NZ)
        return ((there // 2) * NY + y) * NX + x, (there % 2) * 2 + core

    def in_group(d):
        return i, mate(d)

    used = [0]

    def reserve(n=1):
        used[0] += n
        return used[0] - n

    def copy(src, dst, device, at=None, recv_at=None):
        at = reserve() if at is None else at
        recv_at = at if recv_at is None else recv_at
        return pltpu.make_async_remote_copy(
            src_ref=src, dst_ref=dst, send_sem=send.at[at], recv_sem=recv.at[recv_at],
            device_id=device, device_id_type=pl.DeviceIdType.MESH,
        )

    barrier = pltpu.get_barrier_semaphore()
    partners = [in_group(1), in_group(3)]
    partners += [on_x(d) for d in range(1, NX)]
    partners += [on_y(d) for d in range(1, NY)]
    partners += [on_z(d) for d in range(1, 2 * NZ)]
    for device in partners:
        pl.semaphore_signal(barrier, inc=1, device_id=device, device_id_type=pl.DeviceIdType.MESH)
    pl.semaphore_wait(barrier, len(partners))

    sent = []

    def go(c):
        c.start()
        sent.append((None, c))
        return c

    def go_if(cond, cs):
        @pl.when(cond)
        def _():
            for c in cs:
                c.start()

        sent.extend((cond, c) for c in cs)

    def arrived(cs):
        for c in cs:
            c.wait_recv()

    def arrived_if(cond, cs):
        @pl.when(cond)
        def _():
            for c in cs:
                c.wait_recv()

    qall[0, 0] = qg[...]
    ids[0] = jnp.zeros((8, 256), jnp.int32)
    ids[0, :, 0:QD] = jnp.broadcast_to(qid[...], (8, QD))
    core_a = [copy(qall.at[s, 0], qall.at[s, 1], in_group(1)) for s in range(STEPS)]
    core_b = [copy(qall.at[s, 2], qall.at[s, 3], in_group(1)) for s in range(STEPS)]
    z_a = {s: copy(qall.at[s, 0], qall.at[s, 2], in_group(2)) for s in (0, 2)}

    def regroup(half, d):
        rows = pl.ds(pl.multiple_of(mate(d) * PART + half * HALF, HALF), HALF)
        return copy(tg.at[rows, :], xr.at[d - 1, pl.ds(half * HALF, HALF), :], in_group(d))

    regrouped = {(half, d): regroup(half, d) for half in range(2) for d in (2, 3, 1)}

    to_next = [copy(qall.at[0, 2 * n], prev.at[n], on_y(1)) for n in range(2)]
    at_prev_ids = reserve()
    to_next_ids = copy(ids.at[0], prev_ids, on_y(1), None, at_prev_ids)
    wrap_ids_1 = copy(ids.at[0], hop_ids, on_z(2))
    wrap_ids_2 = copy(hop_ids, prev_ids, on_y(1), None, at_prev_ids)
    got = reserve()
    wrap_1 = [
        copy(qall.at[0, 0, :, pl.ds((d - 1) * 128, 128)], hop1, on_y(d), None, got)
        for d in range(1, NY)]
    wrap_2 = [copy(hop1, hop2.at[0], on_z(2)), copy(hop1, hop2.at[1], on_z(3 - 2 * (f // 2)))]
    wrap_3, wrap_in = [], []
    for n in range(2):
        first = reserve(NY)
        at = reserve()
        to_first = (zh * NY * NX + x, f)
        lanes = pl.ds(pl.multiple_of(y * 128, 128), 128)
        wrap_3.append(copy(hop2.at[n], prev.at[n, :, lanes], to_first, at, first + y))
        wrap_in.append([
            copy(hop2.at[n], prev.at[n, :, pl.ds(j * 128, 128)], to_first, at, first + j)
            for j in range(1, NY)])

    def send_next(n):
        go_if(y < NY - 1, [to_next[n]])

    def send_wrap_1():
        go_if(y == NY - 1, wrap_1)

        @pl.when(y == NY - 1)
        def _():
            hop1[...] = qall[0, 0, :, (NY - 1) * 128:NY * 128]

    def send_wrap_2():
        @pl.when(y < NY - 1)
        def _():
            wrap_1[0].wait_recv()

        for c in wrap_2:
            go(c)

    def send_wrap_3():
        arrived(wrap_2)
        go_if(y > 0, wrap_3)

        @pl.when(y == 0)
        def _():
            for n in range(2):
                prev[n, :, 0:128] = hop2[n]

    def wait_prev(n):
        arrived_if(y > 0, [to_next[n]])
        arrived_if(y == 0, wrap_in[n])

    right, left = on_x(1), on_x(NX - 1)
    at_right, at_left, at_relay = reserve(2), reserve(2), reserve(2)
    at_ids = reserve(4)
    own_right = [copy(qall.at[0, 2 * n], qall.at[1, 2 * n], right, at_right + n) for n in range(2)]
    prev_right = [copy(prev.at[n], qall.at[1, 2 * n], right, at_right + n) for n in range(2)]
    own_left = [copy(qall.at[0, 2 * n], qall.at[3, 2 * n], left, at_left + n) for n in range(2)]
    prev_left = [copy(prev.at[n], qall.at[3, 2 * n], left, at_left + n) for n in range(2)]
    own_right_ids = copy(ids.at[0], ids.at[1], right, at_ids)
    prev_right_ids = copy(prev_ids, ids.at[1], right, at_ids)
    own_left_ids = copy(ids.at[0], ids.at[3], left, at_ids + 1)
    prev_left_ids = copy(prev_ids, ids.at[3], left, at_ids + 1)
    relay_r = [copy(qall.at[1, 0], qall.at[2, 0], right, at_relay),
               copy(ids.at[1], ids.at[2], right, at_ids + 2)]
    relay_l = [copy(qall.at[3, 0], qall.at[2, 0], left, at_relay + 1),
               copy(ids.at[3], ids.at[2], left, at_ids + 3)]
    relays = (x == 1) | (x == 2)

    def send_own(n):
        more = n == 0
        go_if(x < NX - 1, [own_right[n]] + [own_right_ids] * more)
        go_if(x == 0, [own_left[n]] + [own_left_ids] * more)

    def send_prev(n):
        more = n == 0
        go_if(x == NX - 1, [prev_right[n]] + [prev_right_ids] * more)
        go_if(x > 0, [prev_left[n]] + [prev_left_ids] * more)

    class Sum:
        def __init__(self, n):
            self.n = n
            self.mine = pl.ds(pl.multiple_of(core * 16, 16), 16)
            self.theirs = pl.ds(pl.multiple_of((1 - core) * 16, 16), 16)
            self.c = copy(packed.at[n, self.theirs, :], c_in.at[n], in_group(1))
            self.x = [copy(part.at[n, 0], x_in.at[n, d - 1], on_x(d)) for d in range(1, NX)]
            self.y = [copy(part.at[n, 1], y_in.at[n, d - 1], on_y(d)) for d in range(1, NY)]
            self.z = [copy(part.at[n, 2], z_in.at[n, d - 1], on_z(d)) for d in range(1, 2 * NZ)]
            self.back = copy(total.at[n], other.at[n], in_group(1))

        def send(self, cs):
            for c in cs:
                go(c)

        def collect(self, cs, first, ref):
            arrived(cs)
            value = first
            for k in range(len(cs)):
                value = value + ref[self.n, k]
            return value

        def start(self):
            go(self.c)

        def start_x(self):
            self.c.wait_recv()
            part[self.n, 0] = packed[self.n, self.mine, :] + c_in[self.n]
            self.send(self.x)

        def start_y(self):
            part[self.n, 1] = self.collect(self.x, part[self.n, 0], x_in)
            self.send(self.y)

        def start_z(self):
            part[self.n, 2] = self.collect(self.y, part[self.n, 1], y_in)
            self.send(self.z)

        def start_back(self):
            total[self.n] = self.collect(self.z, part[self.n, 2], z_in)
            go(self.back)

        def finish(self):
            self.back.wait_recv()
            whole[self.n, self.mine, :] = total[self.n]
            whole[self.n, self.theirs, :] = other[self.n]

    tile = (8, 8, 128)
    lane64 = lax.broadcasted_iota(jnp.int32, (K, 2 * K), 1) % K
    row64 = lax.broadcasted_iota(jnp.int32, (K, 2 * K), 0)
    lane8 = lax.broadcasted_iota(jnp.int32, (8, 2 * K), 1) % K
    row_of = row64.reshape(tile)
    low = lower_lanes(K)

    def invert(n):
        s = whole[n]
        r = pltpu.roll(s, K, 1)
        low32 = lower_lanes(32)
        full = jnp.concatenate([jnp.where(low32, s, r), jnp.where(low32, r, s)], axis=0)
        diag = lane64 == row64
        trace = jnp.sum(jnp.where(diag, full, 0.0)) * 0.5
        mean_total = trace / TRAIN
        inv[n] = full / TRAIN + jnp.where(diag, DAMPING * mean_total / K, 0.0)
        for k in range(0, K, 4):
            a = inv[n]
            spots = [jnp.full((8, 128), k + j, jnp.int32) for j in range(4)]
            rows = [jnp.broadcast_to(inv[n, k + j:k + j + 1, :], (8, 128)) for j in range(4)]
            e = [[jnp.take_along_axis(rows[j], spots[t], axis=1) for t in range(4)] for j in range(4)]
            cols = [
                jnp.take_along_axis(a, jnp.full((K, 128), k + j, jnp.int32), axis=1).reshape(tile)
                for j in range(4)]
            for t in range(4):
                pivot = 1.0 / e[t][t]
                here = lane8 == k + t
                rows[t] = jnp.where(here, 1.0, rows[t]) * pivot
                scaled = [e[t][v] * pivot for v in range(4)]
                for j in range(4):
                    if j != t:
                        rows[j] = jnp.where(here, 0.0, rows[j]) - e[j][t] * rows[t]
                        for v in range(t + 1, 4):
                            e[j][v] = e[j][v] - e[j][t] * scaled[v]
                for v in range(t + 1, 4):
                    e[t][v] = scaled[v]
            inside = (lane8 >= k) & (lane8 < k + 4)
            u = jnp.where(inside[None], 0.0, a.reshape(tile))
            for j in range(4):
                u = u - cols[j] * rows[j][None]
            for j in range(4):
                u = jnp.where(row_of == k + j, rows[j][None], u)
            inv[n] = u.reshape(K, 2 * K)
        return mean_total

    eye = identity(128)
    own_lanes = pl.ds(pl.multiple_of(f * PART, PART), PART)
    rcp_part = 1.0 / cnt[:, own_lanes].astype(F32)

    def transpose(half, d):
        scale = rcp_part[:, half * HALF:(half + 1) * HALF]
        base = mate(d) * (COLS // K * PITCH)
        for k in range(COLS // 128):
            cols = slice(k * 128, (k + 1) * 128)
            if d == 0:
                rows = pl.ds(pl.multiple_of(f * PART + half * HALF, HALF), HALF)
                block = tg[rows, cols]
            else:
                block = xr[d - 1, half * HALF:(half + 1) * HALF, cols]
            t = (dot_nt(eye, block) * scale).astype(BF16).astype(F32)
            for j in range(2):
                xt[half, pl.ds(pl.multiple_of(base + (2 * k + j) * PITCH, 8), K), :] = t[j * K:(j + 1) * K]

    def right_product(s, d):
        base = mate(d) * (COLS // K * PITCH)
        for k in range(COLS // 128):
            t = dot_nt(rsm[...], qall[s, d, :, k * 128:(k + 1) * 128])
            t = t[0:128] + (t[128:256] + t[256:384])
            for j in range(2):
                rows = pl.ds(pl.multiple_of(base + (2 * k + j) * PITCH, 8), K)
                m[0, rows, :] = t[j * K:(j + 1) * K, 0:128]
                m[1, rows, 0:64] = t[j * K:(j + 1) * K, 128:192]

    def prepare(s, pieces):
        for d in pieces:
            right_product(s, d)

        def step(b, carry):
            for d in pieces:
                start = mate(d) * (COLS // K * PITCH)
                at = pl.multiple_of(b * 2 * K + mate(d) * 16, 16)
                for j, lanes in enumerate((128, 64)):
                    hi, lo = split(m[j, pl.ds(start + b, 16, stride=PITCH), :][:, 0:lanes])
                    w[s, pl.ds(at, 16), j * 128:j * 128 + lanes] = hi
                    w[s, pl.ds(at + K, 16), j * 128:j * 128 + lanes] = lo
            return carry

        lax.fori_loop(0, K, step, 0, unroll=8)

    def scores(s):
        def step(b, carry):
            at = pl.multiple_of(b * 128, 128)
            t = dot_nn(lsm[...], w[s, pl.ds(at, 128), :])
            p[pl.ds(pl.multiple_of(b * K, K), K), :] = (t[0:64] + t[64:128]).astype(BF16)
            return carry

        lax.fori_loop(0, K, step, 0, unroll=32)
        value = dot_nn(xbt[...], p[...])
        same = tcol[:, 0:1] == ids[s, 0:1, 0:QD]
        st[s] = jnp.where(same, 0.0, value).T

    results = []

    def hand_out(s):
        for d in (2, 3, 1):
            results.append(go(copy(
                st.at[s, pl.ds(pl.multiple_of(mate(d) * QROWS, 8), QROWS), :],
                out.at[s, :, own_lanes], in_group(d))))
        out[s, :, own_lanes] = st[s, pl.ds(pl.multiple_of(f * QROWS, 8), QROWS), :]

    go(regrouped[0, 2])
    go(core_a[0])
    go(regrouped[0, 1])
    go(regrouped[1, 1])
    send_wrap_1()
    send_next(0)
    go_if(y < NY - 1, [to_next_ids])
    go_if(y == NY - 1, [wrap_ids_1])

    rcp = 1.0 / cnt[...].astype(F32)
    for k in range(COLS // 128):
        t = dot_nt(eye, tg[:, k * 128:(k + 1) * 128])
        xto[k * 128:(k + 1) * 128, :] = (t * rcp).astype(BF16)
    g = jnp.zeros((256, 256), F32)
    for k in range(COLS // 256):
        rows = xto[k * 256:(k + 1) * 256, :]
        g = g + dot_nt(rows, rows)
    packed[0] = fold(g)
    sum0 = Sum(0)
    sum0.start()
    sum0.start_x()
    send_own(0)
    send_wrap_2()
    go(regrouped[0, 3])
    go(regrouped[1, 2])
    go(regrouped[1, 3])
    transpose(0, 0)
    transpose(1, 0)
    tcol[...] = jnp.broadcast_to(tid[:, own_lanes], (128, PART)).T
    sum0.start_y()
    arrived_if(y == NY - 1, [wrap_ids_1])
    go_if(y == NY - 1, [wrap_ids_2])
    send_wrap_3()
    wait_prev(0)
    to_next_ids.wait_recv()
    send_prev(0)
    arrived([regrouped[0, 1], regrouped[1, 1]])
    transpose(0, 1)
    transpose(1, 1)
    sum0.start_z()
    go(z_a[0])
    arrived([regrouped[0, 2], regrouped[0, 3]])
    transpose(0, 2)
    transpose(0, 3)
    arrived([own_right[0], own_left[0], own_right_ids, own_left_ids])
    go_if(relays, relay_r + relay_l)
    go(core_a[1])
    go(core_a[3])

    arrived([regrouped[1, 2], regrouped[1, 3]])
    transpose(1, 2)
    transpose(1, 3)

    def regather(b, carry):
        for half in range(2):
            rows = xt[half, pl.ds(b, K, stride=PITCH), :].astype(BF16)
            xb[pl.ds(pl.multiple_of(b * K, K), K), half * HALF:(half + 1) * HALF] = rows
        return carry

    lax.fori_loop(0, K, regather, 0, unroll=8)

    def add_gram(k, total_g):
        rows = xb[pl.ds(pl.multiple_of(k * 256, 256), 256), :]
        return total_g + dot_nt(rows, rows)

    packed[1] = fold(lax.fori_loop(0, 16, add_gram, jnp.zeros((256, 256), F32), unroll=4))
    sum1 = Sum(1)
    sum1.start()
    sum1.start_x()
    sum0.start_back()
    sum0.finish()
    invert(0)
    full = inv[0]
    hi = full.astype(BF16)
    rest = full - hi.astype(F32)
    mid, tiny = split(rest)
    zero = jnp.zeros_like(hi)
    for n, term in enumerate((hi, mid, tiny)):
        rsm[n * 128:n * 128 + 64, :] = jnp.where(low, term, zero)
        rsm[n * 128 + 64:n * 128 + 128, :] = jnp.where(low, zero, term)
    sum1.start_y()
    z_a[0].wait_recv()
    send_next(1)
    send_own(1)
    go(core_b[0])
    eye256 = identity(256)

    def put_back(k, carry):
        at = pl.multiple_of(k * 256, 256)
        xbt[:, pl.ds(at, 256)] = dot_nt(eye256, xb[pl.ds(at, 256), :]).astype(BF16)
        return carry

    lax.fori_loop(0, 16, put_back, 0, unroll=4)
    sum1.start_z()
    arrived_if(x >= 2, relay_r)
    arrived_if(x < 2, relay_l)
    go(z_a[2])
    go(core_a[2])
    arrived([core_a[0], core_b[0]])
    prepare(0, (0, 1, 2, 3))
    wait_prev(1)
    send_prev(1)
    sum1.start_back()
    arrived([core_a[1], core_a[3]])
    prepare(1, (0, 1))
    sum1.finish()
    mean_total = invert(1)
    hi, lo = split(inv[1] * mean_total)
    lsm[0:64, :] = hi
    lsm[64:128, :] = jnp.where(low, lo, jnp.zeros_like(lo))

    scores(0)
    hand_out(0)
    core_a[2].wait_recv()
    prepare(2, (0, 1))
    z_a[2].wait_recv()
    go(core_b[2])
    prepare(3, (0, 1))
    core_b[2].wait_recv()
    prepare(2, (2, 3))
    arrived([own_right[1], own_left[1]])
    go(core_b[1])
    go(core_b[3])
    scores(2)
    hand_out(2)
    for s in (1, 3):
        core_b[s].wait_recv()
        prepare(s, (2, 3))
        scores(s)
        hand_out(s)

    arrived(results)
    for cond, c in sent:
        if cond is None:
            c.wait_send()
    for cond, c in sent:
        if cond is not None:
            pl.when(cond)(c.wait_send)


N_SEM = 136


def on_device(train_grads, token_counts, train_ids, query_grads, query_ids):
    cnt = token_counts.reshape(1, EX)
    tid = train_ids.reshape(1, EX)
    qid = query_ids.reshape(1, QD)
    vmem = pltpu.VMEM
    scratch = [
        vmem((3, PART, COLS), BF16),
        vmem((COLS, EX), BF16),
        vmem((2, K * PITCH, HALF), F32),
        vmem((K * K, PART), BF16),
        vmem((PART, K * K), BF16),
        vmem((STEPS, NF, QD, COLS), BF16),
        vmem((2, QD, COLS), BF16),
        vmem((QD, 128), BF16),
        vmem((2, QD, 128), BF16),
        vmem((STEPS, 8, 256), jnp.int32),
        vmem((8, 256), jnp.int32),
        vmem((8, 256), jnp.int32),
        vmem((2, K * PITCH, 128), F32),
        vmem((STEPS, 2 * K * K, QD), BF16),
        vmem((STEPS, QD, PART), F32),
        vmem((K * K, QD), BF16),
        vmem((PART, 128), jnp.int32),
        vmem((2, 32, 128), F32),
        vmem((2, 16, 128), F32),
        vmem((2, 3, 16, 128), F32),
        vmem((2, NX - 1, 16, 128), F32),
        vmem((2, NY - 1, 16, 128), F32),
        vmem((2, 2 * NZ - 1, 16, 128), F32),
        vmem((2, 16, 128), F32),
        vmem((2, 16, 128), F32),
        vmem((2, 32, 128), F32),
        vmem((2, K, 2 * K), F32),
        vmem((384, 128), BF16),
        vmem((128, 128), BF16),
        pltpu.SemaphoreType.DMA((N_SEM,)),
        pltpu.SemaphoreType.DMA((N_SEM,)),
    ]
    spec = pl.BlockSpec(memory_space=pltpu.VMEM)
    return pl.pallas_call(
        kernel,
        out_shape=jax.ShapeDtypeStruct((STEPS, QROWS, EX), F32),
        in_specs=[spec] * 5,
        out_specs=spec,
        scratch_shapes=scratch,
        compiler_params=pltpu.CompilerParams(
            collective_id=0, has_side_effects=True, vmem_limit_bytes=58 * 1024 * 1024
        ),
        cost_estimate=pl.CostEstimate(flops=4_000_000_000, bytes_accessed=8_000_000, transcendentals=0),
    )(train_grads, query_grads, cnt, tid, qid)


def solution(mesh):
    in_specs = (P("dp", "feat"), P("dp"), P("dp"), P("dp", "feat"), P("dp"))
    out_specs = P(None, "feat", "dp")
    return jax.shard_map(
        on_device, mesh=mesh, in_specs=in_specs, out_specs=out_specs, check_vma=False
    )
```

```python
import jax
import jax.numpy as jnp
from jax import lax
from jax.experimental import pallas as pl
from jax.experimental.pallas import tpu as pltpu
from jax.sharding import PartitionSpec as P

K = 64
PITCH = 72
STEPS = 4
NX, NY, NZ, NF = 4, 8, 4, 4
N_DP = NX * NY * NZ
TRAIN = 131072
EX = 1024
COLS = 1024
PART = EX // NF
HALF = PART // 2
QD = 192
QROWS = QD // NF
DAMPING = 0.1

F32 = jnp.float32
BF16 = jnp.bfloat16


def dot_nt(a, b):
    return lax.dot_general(a, b, (((1,), (1,)), ((), ())), preferred_element_type=F32)


def dot_nn(a, b):
    return lax.dot_general(a, b, (((1,), (0,)), ((), ())), preferred_element_type=F32)


def identity(n):
    rows = lax.broadcasted_iota(jnp.int32, (n, n), 0)
    cols = lax.broadcasted_iota(jnp.int32, (n, n), 1)
    return jnp.where(rows == cols, 1.0, 0.0).astype(BF16)


def lower_lanes(rows):
    return lax.broadcasted_iota(jnp.int32, (rows, 2 * K), 1) < K


def fold(g):
    low = lower_lanes(K)
    h = jnp.where(low, g[0:64, 0:128], g[64:128, 0:128]) + jnp.where(
        low, g[128:192, 128:256], g[192:256, 128:256]
    )
    both = h + pltpu.roll(h, K, 1)
    return jnp.where(lower_lanes(32), both[0:32], both[32:64])


def split(v):
    high = v.astype(BF16)
    return high, (v - high.astype(F32)).astype(BF16)


def kernel(
    tg, qg, cnt, tid, qid, out,
    xr, xto, xt, xb, xbt, qall, prev, hop1, hop2, ids, prev_ids, hop_ids, m, w, st, p, tcol,
    packed, c_in, part, x_in, y_in, z_in, total, other, whole, inv, rsm, lsm, gram,
    send, recv,
):
    f = lax.axis_index("feat")
    i = lax.axis_index("dp")
    x = i % NX
    y = (i // NX) % NY
    zh = i // (NX * NY)
    core = f % 2
    z = 2 * zh + f // 2

    def mate(d):
        if d == 0:
            return f
        if d == 1:
            return f + 1 - 2 * core
        if d == 2:
            return (f + 2) % 4
        return 3 - f

    def on_x(d):
        return i - x + (x + d) % NX, f

    def on_y(d):
        return (zh * NY + (y + d) % NY) * NX + x, f

    def on_z(d):
        there = (z + d) % (2 * NZ)
        return ((there // 2) * NY + y) * NX + x, (there % 2) * 2 + core

    def in_group(d):
        return i, mate(d)

    used = [0]

    def reserve(n=1):
        used[0] += n
        return used[0] - n

    def copy(src, dst, device, at=None, recv_at=None):
        at = reserve() if at is None else at
        recv_at = at if recv_at is None else recv_at
        return pltpu.make_async_remote_copy(
            src_ref=src, dst_ref=dst, send_sem=send.at[at], recv_sem=recv.at[recv_at],
            device_id=device, device_id_type=pl.DeviceIdType.MESH,
        )

    barrier = pltpu.get_barrier_semaphore()
    partners = [in_group(1), in_group(3)]
    partners += [on_x(d) for d in range(1, NX)]
    partners += [on_y(d) for d in range(1, NY)]
    partners += [on_z(d) for d in range(1, 2 * NZ)]
    for device in partners:
        pl.semaphore_signal(barrier, inc=1, device_id=device, device_id_type=pl.DeviceIdType.MESH)
    pl.semaphore_wait(barrier, len(partners))

    sent = []

    def go(c):
        c.start()
        sent.append((None, c))
        return c

    def go_if(cond, cs):
        @pl.when(cond)
        def _():
            for c in cs:
                c.start()

        sent.extend((cond, c) for c in cs)

    def arrived(cs):
        for c in cs:
            c.wait_recv()

    def arrived_if(cond, cs):
        @pl.when(cond)
        def _():
            for c in cs:
                c.wait_recv()

    qall[0, 0] = qg[...]
    ids[0] = jnp.zeros((8, 256), jnp.int32)
    ids[0, :, 0:QD] = jnp.broadcast_to(qid[...], (8, QD))
    core_a = [copy(qall.at[s, 0], qall.at[s, 1], in_group(1)) for s in range(STEPS)]
    core_b = [copy(qall.at[s, 2], qall.at[s, 3], in_group(1)) for s in range(STEPS)]
    z_a = {s: copy(qall.at[s, 0], qall.at[s, 2], in_group(2)) for s in (0, 2)}

    def regroup(half, d):
        rows = pl.ds(pl.multiple_of(mate(d) * PART + half * HALF, HALF), HALF)
        return copy(tg.at[rows, :], xr.at[d - 1, pl.ds(half * HALF, HALF), :], in_group(d))

    regrouped = {(half, d): regroup(half, d) for half in range(2) for d in (2, 3, 1)}

    to_next = copy(qall.at[0, 0], prev.at[0], on_y(1))
    at_prev_ids = reserve()
    to_next_ids = copy(ids.at[0], prev_ids, on_y(1), None, at_prev_ids)
    wrap_ids_1 = copy(ids.at[0], hop_ids, on_z(2))
    wrap_ids_2 = copy(hop_ids, prev_ids, on_y(1), None, at_prev_ids)
    got = reserve()
    wrap_1 = [
        copy(qall.at[0, 0, :, pl.ds((d - 1) * 128, 128)], hop1, on_y(d), None, got)
        for d in range(1, NY)]
    wrap_2 = [copy(hop1, hop2.at[0], on_z(2)), copy(hop1, hop2.at[1], on_z(3 - 2 * (f // 2)))]
    wrap_3, wrap_in = [], []
    for n in range(2):
        first = reserve(NY)
        at = reserve()
        to_first = (zh * NY * NX + x, f)
        lanes = pl.ds(pl.multiple_of(y * 128, 128), 128)
        wrap_3.append(copy(hop2.at[n], prev.at[n, :, lanes], to_first, at, first + y))
        wrap_in.append([
            copy(hop2.at[n], prev.at[n, :, pl.ds(j * 128, 128)], to_first, at, first + j)
            for j in range(1, NY)])

    def send_wrap_1():
        go_if(y == NY - 1, wrap_1)

        @pl.when(y == NY - 1)
        def _():
            hop1[...] = qall[0, 0, :, (NY - 1) * 128:NY * 128]

    def send_wrap_2():
        @pl.when(y < NY - 1)
        def _():
            wrap_1[0].wait_recv()

        for c in wrap_2:
            go(c)

    def send_wrap_3():
        arrived(wrap_2)
        go_if(y > 0, wrap_3)

        @pl.when(y == 0)
        def _():
            for n in range(2):
                prev[n, :, 0:128] = hop2[n]

    def wait_prev():
        arrived_if(y > 0, [to_next])
        arrived_if(y == 0, wrap_in[0])

    right, left = on_x(1), on_x(NX - 1)
    at_right, at_left, at_relay = reserve(), reserve(), reserve(2)
    at_ids = reserve(4)
    own_right = copy(qall.at[0, 0], qall.at[1, 0], right, at_right)
    prev_right = copy(prev.at[0], qall.at[1, 0], right, at_right)
    own_left = copy(qall.at[0, 0], qall.at[3, 0], left, at_left)
    prev_left = copy(prev.at[0], qall.at[3, 0], left, at_left)
    own_right_ids = copy(ids.at[0], ids.at[1], right, at_ids)
    prev_right_ids = copy(prev_ids, ids.at[1], right, at_ids)
    own_left_ids = copy(ids.at[0], ids.at[3], left, at_ids + 1)
    prev_left_ids = copy(prev_ids, ids.at[3], left, at_ids + 1)
    parts = [pl.ds(0, QD // 2), pl.ds(QD // 2, QD // 2)]
    at_b = reserve(4)
    next_b = [copy(qall.at[0, 2, r, :], prev.at[1, r, :], on_y(1)) for r in parts]
    own_right_b = [copy(qall.at[0, 2, r, :], qall.at[1, 2, r, :], right, at_b + h) for h, r in enumerate(parts)]
    prev_right_b = [copy(prev.at[1, r, :], qall.at[1, 2, r, :], right, at_b + h) for h, r in enumerate(parts)]
    own_left_b = [copy(qall.at[0, 2, r, :], qall.at[3, 2, r, :], left, at_b + 2 + h) for h, r in enumerate(parts)]
    prev_left_b = [copy(prev.at[1, r, :], qall.at[3, 2, r, :], left, at_b + 2 + h) for h, r in enumerate(parts)]

    def pass_prev_b(h):
        arrived_if(y > 0, [next_b[h]])
        if h == 0:
            arrived_if(y == 0, wrap_in[1])
        go_if(x == NX - 1, [prev_right_b[h]])
        go_if(x > 0, [prev_left_b[h]])

    relay_r = [copy(qall.at[1, 0], qall.at[2, 0], right, at_relay),
               copy(ids.at[1], ids.at[2], right, at_ids + 2)]
    relay_l = [copy(qall.at[3, 0], qall.at[2, 0], left, at_relay + 1),
               copy(ids.at[3], ids.at[2], left, at_ids + 3)]
    relays = (x == 1) | (x == 2)

    def send_own():
        go_if(x < NX - 1, [own_right, own_right_ids])
        go_if(x == 0, [own_left, own_left_ids])

    def send_prev():
        go_if(x == NX - 1, [prev_right, prev_right_ids])
        go_if(x > 0, [prev_left, prev_left_ids])

    class Sum:
        def __init__(self, n):
            self.n = n
            self.mine = pl.ds(pl.multiple_of(core * 16, 16), 16)
            self.theirs = pl.ds(pl.multiple_of((1 - core) * 16, 16), 16)
            self.c = copy(packed.at[n, self.theirs, :], c_in.at[n], in_group(1))
            self.x = [copy(part.at[n, 0], x_in.at[n, d - 1], on_x(d)) for d in range(1, NX)]
            self.y = [copy(part.at[n, 1], y_in.at[n, d - 1], on_y(d)) for d in range(1, NY)]
            self.z = [copy(part.at[n, 2], z_in.at[n, d - 1], on_z(d)) for d in range(1, 2 * NZ)]
            self.back = copy(total.at[n], other.at[n], in_group(1))

        def send(self, cs):
            for c in cs:
                go(c)

        def collect(self, cs, first, ref):
            arrived(cs)
            value = first
            for k in range(len(cs)):
                value = value + ref[self.n, k]
            return value

        def start(self):
            go(self.c)

        def start_x(self):
            self.c.wait_recv()
            part[self.n, 0] = packed[self.n, self.mine, :] + c_in[self.n]
            self.send(self.x)

        def start_y(self):
            part[self.n, 1] = self.collect(self.x, part[self.n, 0], x_in)
            self.send(self.y)

        def start_z(self):
            part[self.n, 2] = self.collect(self.y, part[self.n, 1], y_in)
            self.send(self.z)

        def start_back(self):
            total[self.n] = self.collect(self.z, part[self.n, 2], z_in)
            go(self.back)

        def finish(self):
            self.back.wait_recv()
            whole[self.n, self.mine, :] = total[self.n]
            whole[self.n, self.theirs, :] = other[self.n]

    tile = (8, 8, 128)
    lane64 = lax.broadcasted_iota(jnp.int32, (K, 2 * K), 1) % K
    row64 = lax.broadcasted_iota(jnp.int32, (K, 2 * K), 0)
    lane8 = lax.broadcasted_iota(jnp.int32, (8, 2 * K), 1) % K
    row_of = row64.reshape(tile)
    low = lower_lanes(K)

    def invert(n):
        s = whole[n]
        r = pltpu.roll(s, K, 1)
        low32 = lower_lanes(32)
        full = jnp.concatenate([jnp.where(low32, s, r), jnp.where(low32, r, s)], axis=0)
        diag = lane64 == row64
        trace = jnp.sum(jnp.where(diag, full, 0.0)) * 0.5
        mean_total = trace / TRAIN
        inv[n] = full / TRAIN + jnp.where(diag, DAMPING * mean_total / K, 0.0)
        for k in range(0, K, 4):
            a = inv[n]
            spots = [jnp.full((8, 128), k + j, jnp.int32) for j in range(4)]
            rows = [jnp.broadcast_to(inv[n, k + j:k + j + 1, :], (8, 128)) for j in range(4)]
            e = [[jnp.take_along_axis(rows[j], spots[t], axis=1) for t in range(4)] for j in range(4)]
            cols = [
                jnp.take_along_axis(a, jnp.full((K, 128), k + j, jnp.int32), axis=1).reshape(tile)
                for j in range(4)]
            for t in range(4):
                pivot = 1.0 / e[t][t]
                here = lane8 == k + t
                rows[t] = jnp.where(here, 1.0, rows[t]) * pivot
                scaled = [e[t][v] * pivot for v in range(4)]
                for j in range(4):
                    if j != t:
                        rows[j] = jnp.where(here, 0.0, rows[j]) - e[j][t] * rows[t]
                        for v in range(t + 1, 4):
                            e[j][v] = e[j][v] - e[j][t] * scaled[v]
                for v in range(t + 1, 4):
                    e[t][v] = scaled[v]
            inside = (lane8 >= k) & (lane8 < k + 4)
            u = jnp.where(inside[None], 0.0, a.reshape(tile))
            for j in range(4):
                u = u - cols[j] * rows[j][None]
            for j in range(4):
                u = jnp.where(row_of == k + j, rows[j][None], u)
            inv[n] = u.reshape(K, 2 * K)
        return mean_total

    eye = identity(128)
    own_lanes = pl.ds(pl.multiple_of(f * PART, PART), PART)
    rcp_part = 1.0 / cnt[:, own_lanes].astype(F32)

    def transpose(half, d):
        scale = rcp_part[:, half * HALF:(half + 1) * HALF]
        base = mate(d) * (COLS // K * PITCH)
        for k in range(COLS // 128):
            cols = slice(k * 128, (k + 1) * 128)
            if d == 0:
                rows = pl.ds(pl.multiple_of(f * PART + half * HALF, HALF), HALF)
                block = tg[rows, cols]
            else:
                block = xr[d - 1, half * HALF:(half + 1) * HALF, cols]
            t = (dot_nt(eye, block) * scale).astype(BF16).astype(F32)
            for j in range(2):
                xt[half, pl.ds(pl.multiple_of(base + (2 * k + j) * PITCH, 8), K), :] = t[j * K:(j + 1) * K]

    def right_product(s, d):
        base = mate(d) * (COLS // K * PITCH)
        for k in range(COLS // 128):
            t = dot_nt(rsm[...], qall[s, d, :, k * 128:(k + 1) * 128])
            t = t[0:128] + t[128:256]
            for j in range(2):
                rows = pl.ds(pl.multiple_of(base + (2 * k + j) * PITCH, 8), K)
                m[0, rows, :] = t[j * K:(j + 1) * K, 0:128]
                m[1, rows, 0:64] = t[j * K:(j + 1) * K, 128:192]

    def prepare(s, pieces):
        for d in pieces:
            right_product(s, d)

        def step(b, carry):
            for d in pieces:
                start = mate(d) * (COLS // K * PITCH)
                at = pl.multiple_of(b * 2 * K + mate(d) * 16, 16)
                for j, lanes in enumerate((128, 64)):
                    hi, lo = split(m[j, pl.ds(start + b, 16, stride=PITCH), :][:, 0:lanes])
                    first = (s // 2) * 256 + j * 128
                    w[s % 2, pl.ds(at, 16), first:first + lanes] = hi
                    w[s % 2, pl.ds(at + K, 16), first:first + lanes] = lo
            return carry

        lax.fori_loop(0, K, step, 0, unroll=8)

    def scores(pair):
        def step(b, carry):
            t = dot_nn(lsm[...], w[pair, pl.ds(pl.multiple_of(b * 128, 128), 128), :])
            p[pl.ds(pl.multiple_of(b * K, K), K), :] = (t[0:64] + t[64:128]).astype(BF16)
            return carry

        lax.fori_loop(0, K, step, 0, unroll=16)
        value = dot_nn(xbt[...], p[...])
        for s in (pair, pair + 2):
            first = (s // 2) * 256
            same = jnp.concatenate(
                [tcol[...] == ids[s, 0:1, 0:128], tcol[:, 0:QD - 128] == ids[s, 0:1, 128:QD]], axis=1)
            st[s] = jnp.where(same, 0.0, value[:, first:first + QD]).T

    results = []

    def hand_out(s):
        for d in (2, 3, 1):
            results.append(go(copy(
                st.at[s, pl.ds(pl.multiple_of(mate(d) * QROWS, 8), QROWS), :],
                out.at[s, :, own_lanes], in_group(d))))
        out[s, :, own_lanes] = st[s, pl.ds(pl.multiple_of(f * QROWS, 8), QROWS), :]

    go(regrouped[0, 2])
    go(core_a[0])
    go(regrouped[0, 1])
    go(regrouped[1, 1])
    send_wrap_1()
    go_if(y < NY - 1, [to_next])
    go_if(y < NY - 1, [to_next_ids])
    go_if(y == NY - 1, [wrap_ids_1])

    rcp = 1.0 / cnt[...].astype(F32)
    for k in range(COLS // 128):
        t = dot_nt(eye, tg[:, k * 128:(k + 1) * 128])
        xto[k * 128:(k + 1) * 128, :] = (t * rcp).astype(BF16)
    g = jnp.zeros((256, 256), F32)
    for k in range(COLS // 256):
        rows = xto[k * 256:(k + 1) * 256, :]
        g = g + dot_nt(rows, rows)
    packed[0] = fold(g)
    sum0 = Sum(0)
    sum0.start()
    sum0.start_x()
    send_own()
    send_wrap_2()
    go(regrouped[0, 3])
    go(regrouped[1, 2])
    go(regrouped[1, 3])
    transpose(0, 0)
    transpose(1, 0)
    tcol[...] = jnp.broadcast_to(tid[:, own_lanes], (128, PART)).T
    sum0.start_y()
    arrived_if(y == NY - 1, [wrap_ids_1])
    go_if(y == NY - 1, [wrap_ids_2])
    send_wrap_3()
    wait_prev()
    to_next_ids.wait_recv()
    send_prev()
    arrived([regrouped[0, 1], regrouped[1, 1]])
    transpose(0, 1)
    transpose(1, 1)
    sum0.start_z()
    go(z_a[0])
    def regather(half):
        lanes = slice(half * HALF, (half + 1) * HALF)

        def step(b, carry):
            rows = xt[half, pl.ds(b, K, stride=PITCH), :].astype(BF16)
            xb[pl.ds(pl.multiple_of(b * K, K), K), lanes] = rows
            return carry

        lax.fori_loop(0, K, step, 0, unroll=8)

    def add_gram(half, total_g):
        lanes = slice(half * HALF, (half + 1) * HALF)

        def step(k, value):
            rows = xb[pl.ds(pl.multiple_of(k * 256, 256), 256), lanes]
            return value + dot_nt(rows, rows)

        return lax.fori_loop(0, 16, step, total_g, unroll=4)

    arrived([regrouped[0, 2]])
    transpose(0, 2)
    arrived([regrouped[0, 3]])
    transpose(0, 3)
    regather(0)
    gram[...] = add_gram(0, jnp.zeros((256, 256), F32))
    arrived([own_right, own_left, own_right_ids, own_left_ids])
    go_if(relays, relay_r + relay_l)
    go(core_a[1])
    go(core_a[3])

    arrived([regrouped[1, 2]])
    transpose(1, 2)
    arrived([regrouped[1, 3]])
    transpose(1, 3)
    regather(1)
    packed[1] = fold(add_gram(1, gram[...]))
    sum1 = Sum(1)
    sum1.start()
    sum1.start_x()
    sum0.start_back()
    sum0.finish()
    invert(0)
    for n, term in enumerate(split(inv[0])):
        zero = jnp.zeros_like(term)
        rsm[n * 128:n * 128 + 64, :] = jnp.where(low, term, zero)
        rsm[n * 128 + 64:n * 128 + 128, :] = jnp.where(low, zero, term)
    sum1.start_y()
    arrived([core_a[1], core_a[3]])
    prepare(1, (0, 1))
    z_a[0].wait_recv()
    go_if(y < NY - 1, next_b)
    go_if(x < NX - 1, own_right_b)
    go_if(x == 0, own_left_b)
    go(core_b[0])
    prepare(3, (0, 1))
    eye256 = identity(256)

    def put_back(k, carry):
        at = pl.multiple_of(k * 256, 256)
        xbt[:, pl.ds(at, 256)] = dot_nt(eye256, xb[pl.ds(at, 256), :]).astype(BF16)
        return carry

    sum1.start_z()
    arrived_if(x >= 2, relay_r)
    arrived_if(x < 2, relay_l)
    go(z_a[2])
    go(core_a[2])
    lax.fori_loop(0, 16, put_back, 0, unroll=4)
    pass_prev_b(0)
    arrived([core_a[0], core_b[0]])
    prepare(0, (0, 1, 2, 3))
    pass_prev_b(1)
    core_a[2].wait_recv()
    sum1.start_back()
    prepare(2, (0, 1))
    sum1.finish()
    mean_total = invert(1)
    hi, lo = split(inv[1] * mean_total)
    lsm[0:64, :] = hi
    lsm[64:128, :] = jnp.where(low, lo, jnp.zeros_like(lo))

    z_a[2].wait_recv()
    go(core_b[2])
    core_b[2].wait_recv()
    prepare(2, (2, 3))
    arrived(own_right_b + own_left_b)
    go(core_b[1])
    go(core_b[3])
    scores(0)
    hand_out(0)
    hand_out(2)
    for s in (1, 3):
        core_b[s].wait_recv()
        prepare(s, (2, 3))
    scores(1)
    hand_out(1)
    hand_out(3)

    arrived(results)
    for cond, c in sent:
        if cond is None:
            c.wait_send()
    for cond, c in sent:
        if cond is not None:
            pl.when(cond)(c.wait_send)


N_SEM = 136


def on_device(train_grads, token_counts, train_ids, query_grads, query_ids):
    cnt = token_counts.reshape(1, EX)
    tid = train_ids.reshape(1, EX)
    qid = query_ids.reshape(1, QD)
    vmem = pltpu.VMEM
    scratch = [
        vmem((3, PART, COLS), BF16),
        vmem((COLS, EX), BF16),
        vmem((2, K * PITCH, HALF), F32),
        vmem((K * K, PART), BF16),
        vmem((PART, K * K), BF16),
        vmem((STEPS, NF, QD, COLS), BF16),
        vmem((2, QD, COLS), BF16),
        vmem((QD, 128), BF16),
        vmem((2, QD, 128), BF16),
        vmem((STEPS, 8, 256), jnp.int32),
        vmem((8, 256), jnp.int32),
        vmem((8, 256), jnp.int32),
        vmem((2, K * PITCH, 128), F32),
        vmem((2, 2 * K * K, 512), BF16),
        vmem((STEPS, QD, PART), F32),
        vmem((K * K, 512), BF16),
        vmem((PART, 128), jnp.int32),
        vmem((2, 32, 128), F32),
        vmem((2, 16, 128), F32),
        vmem((2, 3, 16, 128), F32),
        vmem((2, NX - 1, 16, 128), F32),
        vmem((2, NY - 1, 16, 128), F32),
        vmem((2, 2 * NZ - 1, 16, 128), F32),
        vmem((2, 16, 128), F32),
        vmem((2, 16, 128), F32),
        vmem((2, 32, 128), F32),
        vmem((2, K, 2 * K), F32),
        vmem((256, 128), BF16),
        vmem((128, 128), BF16),
        vmem((256, 256), F32),
        pltpu.SemaphoreType.DMA((N_SEM,)),
        pltpu.SemaphoreType.DMA((N_SEM,)),
    ]
    spec = pl.BlockSpec(memory_space=pltpu.VMEM)
    return pl.pallas_call(
        kernel,
        out_shape=jax.ShapeDtypeStruct((STEPS, QROWS, EX), F32),
        in_specs=[spec] * 5,
        out_specs=spec,
        scratch_shapes=scratch,
        compiler_params=pltpu.CompilerParams(
            collective_id=0, has_side_effects=True, vmem_limit_bytes=58 * 1024 * 1024
        ),
        cost_estimate=pl.CostEstimate(flops=4_000_000_000, bytes_accessed=8_000_000, transcendentals=0),
    )(train_grads, query_grads, cnt, tid, qid)


def solution(mesh):
    in_specs = (P("dp", "feat"), P("dp"), P("dp"), P("dp", "feat"), P("dp"))
    out_specs = P(None, "feat", "dp")
    return jax.shard_map(
        on_device, mesh=mesh, in_specs=in_specs, out_specs=out_specs, check_vma=False
    )
```
